128 devices in a mesh: list: 8 (over y, core), shard: 16 (over x, z).
Axes of the slice: x: 4, y: 4, z: 4, core: 2. Of those that a mesh axis runs over, the one named last changes fastest.
Arguments:
- embeddings: bfloat16 [262144, 768], P(('list', 'shard')), may hold values from -6 to 6
- list_ids: int32 [262144, 1], P(('list', 'shard')), may hold values from 0 to 15; in each aligned block of 2048 rows (0 to 2047, 2048 to 4095, ...) at most 256 rows name the same one
- centroids: bfloat16 [16, 1024, 768], P('list'), may hold values from -6 to 6
Outputs:
- new_centroids: float32 [16, 1024, 768], P('list', 'shard')
The draws below stay inside these ranges and needn't reach their ends.
Inputs may be any that keep to these rules, and one draw needn't show every extreme that they name: `list_ids`: within each device's 2048 rows no coarse list is named by more than 256 rows, a bound that some block reaches.
All inputs are finite; a program needn't handle non-finite values.
Results may differ from the reference program's by a relative error of at most 0.0014.
Values may be sent and summed in bfloat16 or wider, within the bound.
No kernel may reach another device: no remote copies, remote signals or barrier semaphores. Data moves between devices by JAX's collectives and lax.ppermute only.
A program may use at most 64 MiB of HBM per device.

```python
import math
import jax
import jax.numpy as jnp
import numpy as np
from jax import lax

D = 768
FINE = 1024
R_DEV = 2048
CAP = 256
LISTS = 16
ROWS = 262144
N_LIST = 8
N_SHARD = 16


def block_scale(own_key, extent, pieces, low, largest):
    loudness = 1.0
    for axis_at, shards_of in pieces:
        heights = jax.random.uniform(jax.random.fold_in(jax.random.fold_in(own_key, 6), axis_at), (shards_of,), jnp.float32, low / len(pieces), largest / len(pieces))
        loudness = loudness * jnp.repeat(jnp.exp(heights), extent[axis_at] // shards_of).reshape((-1,) + (1,) * (len(extent) - 1 - axis_at))
    return loudness


def routed_block(rng, own, number, rows, count, top, bound, skew):
    ranking = jax.random.permutation(rng, count)
    packed, usual = load_shares(count, rows * top, bound, skew, True), load_shares(count, rows * top, bound, skew, False)
    places = jnp.arange(count)

    def named(lengths, offset_by):
        used = int((lengths > 0).sum())
        fixed = max(1, used // 4)
        moved = fixed + (places - fixed + offset_by * (used - fixed)) % max(1, count - fixed)
        return jnp.zeros((count,), jnp.int32).at[ranking[jnp.where(places < fixed, places, moved)]].set(jnp.asarray(lengths, jnp.int32))

    lengths = jnp.where(number % 4 == 0, named(packed, number // 4), named(usual, number - number // 4 - 1))
    mixed = jax.random.permutation(jax.random.fold_in(own, 3), count)
    donor, taker = mixed[0:count // 2 * 2:2], mixed[1:count // 2 * 2:2]
    room = jnp.minimum(lengths[donor] - 1, bound - lengths[taker]) // 2
    room = jnp.where((donor == ranking[0]) | (taker == ranking[0]) | (lengths[taker] == 0), 0, jnp.maximum(room, 0))
    moved = jax.random.randint(jax.random.fold_in(own, 4), (count // 2,), 0, 1 << 20) % (room + 1)
    lengths = lengths.at[donor].add(-moved).at[taker].add(moved)
    items = jnp.searchsorted(jnp.cumsum(lengths), jnp.arange(rows * top), side="right").astype(jnp.int32)
    grid = items.reshape(top, rows).T
    grid = grid[jax.random.permutation(jax.random.fold_in(own, 1), rows)]
    offset_by = jax.random.randint(jax.random.fold_in(own, 2), (rows, 1), 0, top)
    return jnp.take_along_axis(grid, (jnp.arange(top)[None, :] + offset_by) % top, axis=1)


def load_shares(amount, total, limit, skew, full):
    portions = [(1 << 20) // math.isqrt(rank ** skew) + 1 for rank in range(1, amount + 1)]
    largest = limit if full else min(limit, max(-(-total // amount), total * portions[0] // sum(portions)))
    least = 1 if total - largest >= amount - 1 else 0
    given, surplus = [largest] + [least] * (amount - 1), total - largest - least * (amount - 1)
    while surplus > 0:
        candidates = [i for i in range(1, amount) if given[i] < largest] or [i for i in range(1, amount) if given[i] < limit]
        pool, budget = sum([portions[i] for i in candidates]), surplus
        for i in candidates:
            more = min(limit - given[i], max(1, budget * portions[i] // pool), surplus)
            given[i] = given[i] + more
            surplus = surplus - more
    return np.array(given)


def noise(stream_key, extent, spread, most, split=(), held_as=jnp.bfloat16):
    drawn = spread * jax.random.normal(stream_key, extent, jnp.float32)
    if split:
        drawn = drawn * block_scale(stream_key, extent, split, -0.22, 0.18)
    return jnp.clip(drawn, -most, most).astype(held_as)


def setup_inputs(seed: int = 0) -> dict:
    streams_of = jax.random.split(jax.random.key(seed), 4)
    embeddings = noise(streams_of[0], (ROWS, D), 1.0, 6.0, ((0, 128),))
    list_ids_keys = jax.random.split(jax.random.fold_in(streams_of[1], 1), ROWS // R_DEV)
    list_ids_turns = jax.random.permutation(jax.random.fold_in(streams_of[1], 3), ROWS // R_DEV)
    list_ids = jax.vmap(lambda own, number: routed_block(jax.random.fold_in(streams_of[1], 2), own, number, R_DEV, LISTS, 1, CAP, 2))(list_ids_keys, list_ids_turns).reshape((ROWS, 1))
    centroids = noise(streams_of[2], (LISTS, FINE, D), 1.0, 6.0, ((0, 8),))
    return dict(embeddings=embeddings, list_ids=list_ids, centroids=centroids)


SHARP = 0.1
PRIOR = 1.0


def list_stats(block, live, cents):
    raw = jnp.dot(block, cents.T, preferred_element_type=jnp.float32)
    cent_sq = jnp.sum(jnp.square(cents.astype(jnp.float32)), axis=1)
    scores = SHARP * raw - 0.5 * SHARP * cent_sq[None, :]
    resp = jax.nn.softmax(scores, axis=-1) * live[:, None]
    resp = resp.astype(jnp.bfloat16)
    sums = jnp.dot(resp.T, block, preferred_element_type=jnp.float32)
    mass = jnp.sum(resp.astype(jnp.float32), axis=0)
    return sums, mass


def reference(embeddings, list_ids, centroids):
    ids = list_ids[:, 0]
    width = N_LIST * N_SHARD * CAP
    order = jnp.argsort(ids, stable=True)
    ordered = embeddings[order]
    padded = jnp.concatenate([ordered, jnp.zeros((width, D), jnp.bfloat16)], axis=0)
    counts = jnp.sum((ids[:, None] == jnp.arange(LISTS, dtype=jnp.int32)[None, :]).astype(jnp.int32), axis=0)
    starts = (jnp.cumsum(counts) - counts).astype(jnp.int32)

    def one_list(index):
        block = lax.dynamic_slice_in_dim(padded, starts[index], width, 0)
        live = (jnp.arange(width, dtype=jnp.int32) < counts[index]).astype(jnp.float32)
        cents = centroids[index]
        sums, mass = list_stats(block, live, cents)
        return (sums + PRIOR * cents.astype(jnp.float32)) / (mass[:, None] + PRIOR)

    return lax.map(one_list, jnp.arange(LISTS, dtype=jnp.int32))
```

```python
import functools
import math

import jax
import jax.numpy as jnp
from jax import lax
from jax.experimental import pallas as pl
from jax.experimental.pallas import tpu as pltpu
from jax.sharding import PartitionSpec as P

SHARP = 0.1
PRIOR = 1.0
LOG2E = math.log2(math.e)
LANES = 128
PAD_MARK = 64.0
PAD_TEST = 32.0
TAIL_ROWS = 16
HOPS = ((0, 0), (0, 1), (1, 0), (3, 0), (1, 1), (3, 1), (2, 0), (2, 1))
STAGES = ((0, 4), (4, 6), (6, 8))
VMEM = pl.BlockSpec(memory_space=pltpu.VMEM)
SMEM = pl.BlockSpec(memory_space=pltpu.SMEM)
PARAMS = pltpu.CompilerParams(vmem_limit_bytes=48 * 2**20)


def pack_kernel(lists, cap, index, dest_ref, ids_ref, rows_ref, *rest):
    outs, (key_ref, count_ref) = rest[:-2], rest[-2:]
    local = lists // len(outs)
    row_count = ids_ref.shape[1]
    names = lax.broadcasted_iota(jnp.int32, (lists, LANES), 0)
    earlier = lax.broadcasted_iota(jnp.int32, (LANES, LANES), 0) < lax.broadcasted_iota(jnp.int32, (LANES, LANES), 1)
    earlier = jnp.where(earlier, 1.0, 0.0).astype(jnp.bfloat16)
    seen = jnp.zeros((lists, 1), jnp.float32)
    for b in range(row_count // LANES):
        hit = ids_ref[:, b * LANES : (b + 1) * LANES] == names
        hot = jnp.where(hit, 1.0, 0.0)
        before = jnp.dot(hot.astype(jnp.bfloat16), earlier, preferred_element_type=jnp.float32) + seen
        key_ref[:, b * LANES : (b + 1) * LANES] = jnp.where(hit, before, -1.0).astype(jnp.int32)
        seen = seen + jnp.sum(hot, axis=1, keepdims=True)
    count_ref[...] = jnp.broadcast_to(seen, (lists, LANES)).astype(jnp.int32)
    slots = lax.broadcasted_iota(jnp.int32, (cap, row_count), 0)
    lane = lax.broadcasted_iota(jnp.int32, (cap, LANES), 1)
    slot = lax.broadcasted_iota(jnp.int32, (cap, LANES), 0)
    for k, out_ref in enumerate(outs):
        name = dest_ref[k] * local + index
        pick = jnp.where(key_ref[pl.ds(name, 1), :] == slots, 1.0, 0.0).astype(jnp.bfloat16)
        out = jnp.dot(pick, rows_ref[...], preferred_element_type=jnp.float32)
        out_ref[...] = out.astype(jnp.bfloat16)
        padding = (lane == 0) & (slot >= count_ref[pl.ds(name, 1), :])
        out_ref[:, :LANES] = jnp.where(padding, PAD_MARK, out[:, :LANES]).astype(jnp.bfloat16)


def pack(dest, ids, rows, lists, cap, index):
    width = rows.shape[1]
    groups = dest.shape[0]
    return pl.pallas_call(
        functools.partial(pack_kernel, lists, cap, index),
        out_shape=[jax.ShapeDtypeStruct((cap, width), jnp.bfloat16)] * groups,
        in_specs=[SMEM, VMEM, VMEM],
        out_specs=[VMEM] * groups,
        scratch_shapes=[pltpu.VMEM((lists, rows.shape[0]), jnp.int32), pltpu.VMEM((lists, LANES), jnp.int32)],
        compiler_params=PARAMS,
        cost_estimate=pl.CostEstimate(
            flops=2 * groups * cap * rows.shape[0] * width, bytes_accessed=2 * 3 * rows.size, transcendentals=0
        ),
        name=f"pack_{index}",
    )(dest, ids, rows)


def norm_kernel(cents_ref, out_ref):
    c = cents_ref[...].astype(jnp.float32)
    total = jnp.sum(jnp.square(c), axis=1, keepdims=True) * (0.5 * SHARP * LOG2E)
    out_ref[...] = jnp.broadcast_to(total, out_ref.shape)


def norms(cents, index):
    _, fine, width = cents.shape
    return pl.pallas_call(
        norm_kernel,
        out_shape=jax.ShapeDtypeStruct((fine, LANES), jnp.float32),
        grid=(1,),
        in_specs=[pl.BlockSpec((None, fine, width), lambda _: (index, 0, 0))],
        out_specs=pl.BlockSpec((fine, LANES), lambda _: (0, 0)),
        compiler_params=PARAMS,
        name=f"norms_{index}",
    )(cents)


def stats_kernel(blocks, carried, last, shares, *refs):
    cents_ref, norm_ref = refs[:2]
    row_refs = refs[2 : 2 + blocks]
    refs = refs[2 + blocks :]
    if carried:
        old_sums_ref, old_mass_ref = refs[:2]
        refs = refs[2:]
    if last:
        out_ref, sums_ref = refs
    else:
        sums_ref, mass_ref = refs
    fine = cents_ref.shape[0]
    mass = old_mass_ref[...] if carried else jnp.zeros((fine, LANES), jnp.float32)
    for n, rows_ref in enumerate(row_refs):
        rows = rows_ref[...]
        cap = rows.shape[0]
        raw = lax.dot_general(cents_ref[...], rows, (((1,), (1,)), ((), ())), preferred_element_type=jnp.float32)
        norm = jnp.concatenate([norm_ref[...]] * (cap // LANES), axis=1)
        scores = raw * (SHARP * LOG2E) - norm
        p = jnp.exp2(scores - jnp.max(scores, axis=0, keepdims=True))
        mark = jnp.transpose(rows[:, :LANES].astype(jnp.float32))[0:1, :]
        scale = jnp.where(mark < PAD_TEST, 1.0, 0.0) / jnp.sum(p, axis=0, keepdims=True)
        resp = (p * scale).astype(jnp.bfloat16)
        back = resp.astype(jnp.float32)
        for j in range(cap // LANES):
            mass = mass + back[:, j * LANES : (j + 1) * LANES]
        part = jnp.dot(resp, rows, preferred_element_type=jnp.float32)
        if n > 0:
            sums_ref[...] += part
        elif carried:
            sums_ref[...] = old_sums_ref[...] + part
        else:
            sums_ref[...] = part
    if not last:
        mass_ref[...] = mass
        return
    share = fine // shares
    groups = sums_ref.shape[1] // LANES
    line = jnp.sum(jnp.transpose(mass), axis=0, keepdims=True)
    high = line.astype(jnp.bfloat16).astype(jnp.float32)
    low = line - high
    row = lax.broadcasted_iota(jnp.int32, (TAIL_ROWS, LANES), 0)
    for s in range(shares):
        for j in range(groups):
            part = sums_ref[s * share : (s + 1) * share, j * LANES : (j + 1) * LANES]
            out_ref[s, j * share : (j + 1) * share, :] = part.astype(jnp.bfloat16)
        at = s * share // LANES * LANES
        tail = jnp.where(row == 0, high[:, at : at + LANES], jnp.where(row == 1, low[:, at : at + LANES], 0.0))
        out_ref[s, groups * share :, :] = tail.astype(jnp.bfloat16)


def stats(cents, index, norm, rows, carried, last, shares):
    _, fine, width = cents.shape
    sums = jax.ShapeDtypeStruct((fine, width), jnp.float32)
    mass = jax.ShapeDtypeStruct((fine, LANES), jnp.float32)
    sent = jax.ShapeDtypeStruct((shares, fine // shares * (width // LANES) + TAIL_ROWS, LANES), jnp.bfloat16)
    whole = lambda shape: pl.BlockSpec(shape, lambda _: (0,) * len(shape))
    operands = [cents, norm, *rows, *(carried or ())]
    specs = [pl.BlockSpec((None, fine, width), lambda _: (index, 0, 0))] + [whole(a.shape) for a in operands[1:]]
    count = sum(r.shape[0] for r in rows)
    return pl.pallas_call(
        functools.partial(stats_kernel, len(rows), carried is not None, last, shares),
        out_shape=sent if last else [sums, mass],
        grid=(1,),
        in_specs=specs,
        out_specs=whole(sent.shape) if last else [whole(sums.shape), whole(mass.shape)],
        scratch_shapes=[pltpu.VMEM(sums.shape, jnp.float32)] if last else [],
        compiler_params=PARAMS,
        cost_estimate=pl.CostEstimate(
            flops=4 * count * fine * width, bytes_accessed=2 * fine * width * 5, transcendentals=count * fine
        ),
        name=f"stats_{index}",
    )(*operands)


def finish_kernel(me_ref, got_ref, cents_ref, *rest):
    out_ref, mass_ref = rest[-2:]
    share, width = out_ref.shape
    total = got_ref[0].astype(jnp.float32)
    for k in range(1, got_ref.shape[0]):
        total = total + got_ref[k].astype(jnp.float32)
    groups = width // LANES
    line = total[groups * share : groups * share + 1, :] + total[groups * share + 1 : groups * share + 2, :]
    mass_ref[...] = jnp.transpose(jnp.broadcast_to(line, (LANES, LANES)))
    offset = lax.rem(me_ref[0] * share, LANES)
    mass = mass_ref[pl.ds(pl.multiple_of(offset, share), share), :] + PRIOR
    for j in range(groups):
        own = cents_ref[:, j * LANES : (j + 1) * LANES].astype(jnp.float32)
        out_ref[:, j * LANES : (j + 1) * LANES] = (total[j * share : (j + 1) * share, :] + PRIOR * own) / mass


def finish(me, got, cents, index, sofar):
    local, fine, width = cents.shape
    share = fine // got.shape[0]
    operands = [got, cents] + ([] if sofar is None else [sofar])
    return pl.pallas_call(
        finish_kernel,
        out_shape=jax.ShapeDtypeStruct((local, share, width), jnp.float32),
        grid_spec=pltpu.PrefetchScalarGridSpec(
            num_scalar_prefetch=1,
            grid=(1,),
            in_specs=[
                pl.BlockSpec(got.shape, lambda _, me: (0, 0, 0)),
                pl.BlockSpec((None, share, width), lambda _, me: (index, me[0], 0)),
            ]
            + ([] if sofar is None else [pl.BlockSpec(memory_space=pl.ANY)]),
            out_specs=pl.BlockSpec((None, share, width), lambda _, me: (index, 0, 0)),
            scratch_shapes=[pltpu.VMEM((LANES, LANES), jnp.float32)],
        ),
        input_output_aliases={} if sofar is None else {3: 0},
        compiler_params=PARAMS,
        name=f"finish_{index}",
    )(me, *operands)


def hop(block, step, groups):
    dy, dc = step
    if (dy, dc) == (0, 0):
        return block
    pairs = [(g, (g // 2 + dy) % (groups // 2) * 2 + (g % 2 ^ dc)) for g in range(groups)]
    return lax.ppermute(block, "list", pairs)


def per_device(embeddings, list_ids, centroids):
    groups = lax.axis_size("list")
    shares = lax.axis_size("shard")
    local = centroids.shape[0]
    lists = local * groups
    cap = embeddings.shape[0] // 8
    ids = list_ids.reshape(1, -1)
    g = lax.axis_index("list").astype(jnp.int32)
    me = lax.axis_index("shard").astype(jnp.int32).reshape(1)
    dest = jnp.stack([(g // 2 + dy) % (groups // 2) * 2 + (g % 2 ^ dc) for dy, dc in HOPS])
    out = None
    for index in range(local):
        sent = pack(dest, ids, embeddings, lists, cap, index)
        rows = [hop(b, step, groups) for b, step in zip(sent, HOPS)]
        norm = norms(centroids, index)
        carried = None
        for first, end in STAGES:
            last = end == groups
            carried = stats(centroids, index, norm, rows[first:end], carried, last, shares)
        got = lax.all_to_all(carried, "shard", split_axis=0, concat_axis=0, tiled=True)
        out = finish(me, got, centroids, index, out)
    return out


def solution(mesh):
    placed = (P(("list", "shard"), None), P(("list", "shard"), None), P("list", None, None))
    return jax.shard_map(
        per_device, mesh=mesh, in_specs=placed, out_specs=P("list", "shard", None), check_vma=False
    )
```

```python
import functools
import math

import jax
import jax.numpy as jnp
import numpy as np
from jax import lax
from jax.experimental import pallas as pl
from jax.experimental.pallas import tpu as pltpu
from jax.sharding import PartitionSpec as P

SHARP = 0.1
PRIOR = 1.0
LOG2E = math.log2(math.e)
LANES = 128
PAD_MARK = 64.0
PAD_TEST = 32.0
TAIL_ROWS = 16
PIECES = 4
HOPS = ((1, 0), (3, 0), (1, 1), (3, 1), (2, 0), (2, 1), (0, 1), (0, 0))
STAGES = ((7, 0, 1), (2, 3, 6), (4, 5))
FIRST = 2
VMEM = pl.BlockSpec(memory_space=pltpu.VMEM)
SMEM = pl.BlockSpec(memory_space=pltpu.SMEM)
PARAMS = pltpu.CompilerParams(vmem_limit_bytes=48 * 2**20)


def count_into(key_ref, count_ref, ids_ref):
    lists = key_ref.shape[0]
    names = lax.broadcasted_iota(jnp.int32, (lists, LANES), 0)
    earlier = lax.broadcasted_iota(jnp.int32, (LANES, LANES), 0) < lax.broadcasted_iota(jnp.int32, (LANES, LANES), 1)
    earlier = jnp.where(earlier, 1.0, 0.0).astype(jnp.bfloat16)
    seen = jnp.zeros((lists, 1), jnp.float32)
    for b in range(ids_ref.shape[1] // LANES):
        hit = ids_ref[:, b * LANES : (b + 1) * LANES] == names
        hot = jnp.where(hit, 1.0, 0.0)
        before = jnp.dot(hot.astype(jnp.bfloat16), earlier, preferred_element_type=jnp.float32) + seen
        key_ref[:, b * LANES : (b + 1) * LANES] = jnp.where(hit, before, -1.0).astype(jnp.int32)
        seen = seen + jnp.sum(hot, axis=1, keepdims=True)
    count_ref[...] = jnp.broadcast_to(seen, count_ref.shape).astype(jnp.int32)


def pack_kernel(first, at, *refs):
    if first:
        names_ref, ids_ref, rows_ref, key_ref, count_ref, *outs = refs
        count_into(key_ref, count_ref, ids_ref)
    else:
        names_ref, rows_ref, key_ref, count_ref, *outs = refs
    cap = outs[0].shape[0]
    slots = lax.broadcasted_iota(jnp.int32, (cap, rows_ref.shape[0]), 0)
    lane = lax.broadcasted_iota(jnp.int32, (cap, LANES), 1)
    slot = lax.broadcasted_iota(jnp.int32, (cap, LANES), 0)
    for k, out_ref in enumerate(outs):
        name = names_ref[at + k]
        pick = jnp.where(key_ref[pl.ds(name, 1), :] == slots, 1.0, 0.0).astype(jnp.bfloat16)
        out = jnp.dot(pick, rows_ref[...], preferred_element_type=jnp.float32)
        out_ref[...] = out.astype(jnp.bfloat16)
        padding = (lane == 0) & (slot >= count_ref[pl.ds(name, 1), :])
        out_ref[:, :LANES] = jnp.where(padding, PAD_MARK, out[:, :LANES]).astype(jnp.bfloat16)


def pack(names, at, blocks, rows, lists, cap, ids=None, keys=None):
    count, width = rows.shape
    made = [jax.ShapeDtypeStruct((cap, width), jnp.bfloat16)] * blocks
    kept = [jax.ShapeDtypeStruct((lists, count), jnp.int32), jax.ShapeDtypeStruct((lists, LANES), jnp.int32)]
    operands = [names] + ([ids, rows] if keys is None else [rows, *keys])
    made = (kept if keys is None else []) + made
    out = pl.pallas_call(
        functools.partial(pack_kernel, keys is None, at),
        out_shape=made,
        in_specs=[SMEM] + [VMEM] * (len(operands) - 1),
        out_specs=[VMEM] * len(made),
        compiler_params=PARAMS,
        cost_estimate=pl.CostEstimate(
            flops=2 * blocks * cap * count * width, bytes_accessed=2 * rows.size, transcendentals=0
        ),
        name="pack",
    )(*operands)
    out = list(out)
    return (out[:2], out[2:]) if keys is None else out


def norm_kernel(cents_ref, *outs):
    for index, out_ref in enumerate(outs):
        c = cents_ref[index].astype(jnp.float32)
        total = jnp.sum(jnp.square(c), axis=1, keepdims=True) * (0.5 * SHARP * LOG2E)
        out_ref[...] = jnp.broadcast_to(total, out_ref.shape)


def norms(cents):
    local, fine, _ = cents.shape
    return pl.pallas_call(
        norm_kernel,
        out_shape=[jax.ShapeDtypeStruct((fine, LANES), jnp.float32)] * local,
        in_specs=[VMEM],
        out_specs=[VMEM] * local,
        compiler_params=PARAMS,
        name="norms",
    )(cents)


def responses(cents_ref, index, norm_ref, rows):
    cap = rows.shape[0]
    raw = lax.dot_general(cents_ref[index], rows, (((1,), (1,)), ((), ())), preferred_element_type=jnp.float32)
    norm = jnp.concatenate([norm_ref[...]] * (cap // LANES), axis=1)
    scores = raw * (SHARP * LOG2E) - norm
    p = jnp.exp2(scores - jnp.max(scores, axis=0, keepdims=True))
    mark = jnp.transpose(rows[:, :LANES].astype(jnp.float32))[0:1, :]
    scale = jnp.where(mark < PAD_TEST, 1.0, 0.0) / jnp.sum(p, axis=0, keepdims=True)
    resp = (p * scale).astype(jnp.bfloat16)
    back = resp.astype(jnp.float32)
    mass = back[:, :LANES]
    for j in range(1, cap // LANES):
        mass = mass + back[:, j * LANES : (j + 1) * LANES]
    return resp, mass


def stats_kernel(index, blocks, carried, *refs):
    cents_ref, norm_ref = refs[:2]
    row_refs = refs[2 : 2 + blocks]
    sums_ref, mass_ref = refs[-2:]
    for n, rows_ref in enumerate(row_refs):
        rows = rows_ref[...]
        resp, mass = responses(cents_ref, index, norm_ref, rows)
        part = jnp.dot(resp, rows, preferred_element_type=jnp.float32)
        if n > 0:
            sums_ref[...] += part
            mass_ref[...] += mass
        elif carried:
            sums_ref[...] = refs[2 + blocks][...] + part
            mass_ref[...] = refs[3 + blocks][...] + mass
        else:
            sums_ref[...] = part
            mass_ref[...] = mass


def last_kernel(index, blocks, shares, *refs):
    cents_ref, norm_ref = refs[:2]
    row_refs = refs[2 : 2 + blocks]
    sums_ref, mass_ref, out_ref, old_ref, send_ref, resp_ref, in_sem, out_sem = refs[2 + blocks :]
    load = pltpu.make_async_copy(sums_ref, old_ref, in_sem)
    load.start()
    fine, width = old_ref.shape
    share = fine // shares
    groups = width // LANES
    total = mass_ref[...]
    for n, rows_ref in enumerate(row_refs):
        resp, mass = responses(cents_ref, index, norm_ref, rows_ref[...])
        resp_ref[n] = resp
        total = total + mass
    line = jnp.sum(jnp.transpose(total), axis=0, keepdims=True)
    high = line.astype(jnp.bfloat16).astype(jnp.float32)
    low = line - high
    row = lax.broadcasted_iota(jnp.int32, (TAIL_ROWS, LANES), 0)
    load.wait()
    copies = []
    per = shares // PIECES
    for piece in range(PIECES):
        at = piece * per * share
        part = old_ref[at : at + per * share, :]
        for n, rows_ref in enumerate(row_refs):
            part += jnp.dot(resp_ref[n, at : at + per * share, :], rows_ref[...], preferred_element_type=jnp.float32)
        for t in range(per):
            s = piece * per + t
            for j in range(groups):
                some = part[t * share : (t + 1) * share, j * LANES : (j + 1) * LANES]
                send_ref[s, j * share : (j + 1) * share, :] = some.astype(jnp.bfloat16)
            where = s * share // LANES * LANES
            both = jnp.where(row == 0, high[:, where : where + LANES], jnp.where(row == 1, low[:, where : where + LANES], 0.0))
            send_ref[s, groups * share :, :] = both.astype(jnp.bfloat16)
        rng = pl.ds(piece * per, per)
        copies.append(pltpu.make_async_copy(send_ref.at[rng], out_ref.at[rng], out_sem.at[piece]))
        copies[-1].start()
    for copy in copies:
        copy.wait()


def stats(cents, index, norm, rows, carried):
    _, fine, width = cents.shape
    sums = jax.ShapeDtypeStruct((fine, width), jnp.float32)
    mass = jax.ShapeDtypeStruct((fine, LANES), jnp.float32)
    operands = [cents, norm, *rows, *(carried or ())]
    return pl.pallas_call(
        functools.partial(stats_kernel, index, len(rows), carried is not None),
        out_shape=[sums, mass],
        in_specs=[VMEM] * len(operands),
        out_specs=[VMEM, VMEM],
        compiler_params=PARAMS,
        name=f"stats_{index}",
    )(*operands)


def last_stats(cents, index, norm, rows, carried, shares):
    _, fine, width = cents.shape
    sent = (shares, fine // shares * (width // LANES) + TAIL_ROWS, LANES)
    operands = [cents, norm, *rows, *carried]
    return pl.pallas_call(
        functools.partial(last_kernel, index, len(rows), shares),
        out_shape=jax.ShapeDtypeStruct(sent, jnp.bfloat16),
        in_specs=[VMEM] * (2 + len(rows)) + [pl.BlockSpec(memory_space=pl.ANY), VMEM],
        out_specs=pl.BlockSpec(memory_space=pl.ANY),
        scratch_shapes=[
            pltpu.VMEM((fine, width), jnp.float32),
            pltpu.VMEM(sent, jnp.bfloat16),
            pltpu.VMEM((len(rows), fine, rows[0].shape[0]), jnp.bfloat16),
            pltpu.SemaphoreType.DMA,
            pltpu.SemaphoreType.DMA((PIECES,)),
        ],
        compiler_params=PARAMS,
        name=f"last_{index}",
    )(*operands)


def finish_kernel(me_ref, got_ref, cents_ref, *rest):
    out_ref, mass_ref = rest[-2:]
    share, width = out_ref.shape
    total = got_ref[0].astype(jnp.float32)
    for k in range(1, got_ref.shape[0]):
        total = total + got_ref[k].astype(jnp.float32)
    groups = width // LANES
    line = total[groups * share : groups * share + 1, :] + total[groups * share + 1 : groups * share + 2, :]
    mass_ref[...] = jnp.transpose(jnp.broadcast_to(line, (LANES, LANES)))
    offset = lax.rem(me_ref[0] * share, LANES)
    mass = mass_ref[pl.ds(pl.multiple_of(offset, share), share), :] + PRIOR
    for j in range(groups):
        own = cents_ref[:, j * LANES : (j + 1) * LANES].astype(jnp.float32)
        out_ref[:, j * LANES : (j + 1) * LANES] = (total[j * share : (j + 1) * share, :] + PRIOR * own) / mass


def finish(me, got, cents, index, sofar):
    local, fine, width = cents.shape
    share = fine // got.shape[0]
    operands = [got, cents] + ([] if sofar is None else [sofar])
    return pl.pallas_call(
        finish_kernel,
        out_shape=jax.ShapeDtypeStruct((local, share, width), jnp.float32),
        grid_spec=pltpu.PrefetchScalarGridSpec(
            num_scalar_prefetch=1,
            grid=(1,),
            in_specs=[
                pl.BlockSpec(got.shape, lambda _, me: (0, 0, 0)),
                pl.BlockSpec((None, share, width), lambda _, me: (index, me[0], 0)),
            ]
            + ([] if sofar is None else [pl.BlockSpec(memory_space=pl.ANY)]),
            out_specs=pl.BlockSpec((None, share, width), lambda _, me: (index, 0, 0)),
            scratch_shapes=[pltpu.VMEM((LANES, LANES), jnp.float32)],
        ),
        input_output_aliases={} if sofar is None else {3: 0},
        compiler_params=PARAMS,
        name=f"finish_{index}",
    )(me, *operands)


def target(g, step, groups):
    return (g // 2 + step[0]) % (groups // 2) * 2 + (g % 2 ^ step[1])


def hop(block, step, groups):
    if step == (0, 0):
        return block
    return lax.ppermute(block, "list", [(g, target(g, step, groups)) for g in range(groups)])


def per_device(embeddings, list_ids, centroids):
    groups = lax.axis_size("list")
    shares = lax.axis_size("shard")
    local = centroids.shape[0]
    lists = local * groups
    cap = embeddings.shape[0] // 8
    ids = list_ids.reshape(1, -1)
    g = lax.axis_index("list").astype(jnp.int32)
    me = lax.axis_index("shard").astype(jnp.int32).reshape(1)
    table = [[target(k, step, groups) for step in HOPS] for k in range(groups)]
    table = np.array([[d * local + i for i in range(local) for d in row] for row in table], np.int32)
    names = lax.dynamic_index_in_dim(jnp.asarray(table), g, 0, keepdims=False)
    tie = lax.optimization_barrier
    keys, sent = pack(names, 0, FIRST, embeddings, lists, cap, ids=ids)
    sent = sent + pack(names, FIRST, groups - FIRST, embeddings, lists, cap, keys=keys)
    later = pack(names, groups, groups, embeddings, lists, cap, keys=keys)
    sent[-1], later = tie((sent[-1], later))
    norm = norms(centroids)
    rows = [[hop(b, step, groups) for b, step in zip(blocks, HOPS)] for blocks in (sent, later)]

    def some(index, stage):
        return [rows[index][k] for k in STAGES[stage]]

    carried = stats(centroids, 0, norm[0], some(0, 0), None)
    carried = stats(centroids, 0, norm[0], some(0, 1), carried)
    part = last_stats(centroids, 0, norm[0], some(0, 2), carried, shares)
    part, rows[1][0], rows[1][1] = tie((part, rows[1][0], rows[1][1]))
    got = lax.all_to_all(part, "shard", split_axis=0, concat_axis=0, tiled=True)
    carried = stats(centroids, 1, norm[1], some(1, 0), None)
    carried = stats(centroids, 1, norm[1], some(1, 1), carried)
    part = last_stats(centroids, 1, norm[1], some(1, 2), carried, shares)
    out = finish(me, got, centroids, 0, None)
    got = lax.all_to_all(part, "shard", split_axis=0, concat_axis=0, tiled=True)
    return finish(me, got, centroids, 1, out)


def solution(mesh):
    placed = (P(("list", "shard"), None), P(("list", "shard"), None), P("list", None, None))
    return jax.shard_map(
        per_device, mesh=mesh, in_specs=placed, out_specs=P("list", "shard", None), check_vma=False
    )
```

```python
import functools
import math

import jax
import jax.numpy as jnp
import numpy as np
from jax import lax
from jax.experimental import pallas as pl
from jax.experimental.pallas import tpu as pltpu
from jax.sharding import PartitionSpec as P

SHARP = 0.1
PRIOR = 1.0
LOG2E = math.log2(math.e)
LANES = 128
PAD_MARK = 64.0
PAD_TEST = 32.0
TAIL_ROWS = 16
PIECES = 4
HOPS = ((1, 0), (3, 0), (1, 1), (3, 1), (2, 0), (2, 1), (0, 1), (0, 0))
STAGES = (((7, 0, 1), (2, 3, 6), (4, 5)), ((7, 0, 1, 2, 3), (4, 5, 6)))
TIED = 4
FIRST = 2
VMEM = pl.BlockSpec(memory_space=pltpu.VMEM)
SMEM = pl.BlockSpec(memory_space=pltpu.SMEM)
PARAMS = pltpu.CompilerParams(vmem_limit_bytes=20 * 2**20)


def count_into(key_ref, count_ref, ids_ref):
    lists = key_ref.shape[0]
    names = lax.broadcasted_iota(jnp.int32, (lists, LANES), 0)
    earlier = lax.broadcasted_iota(jnp.int32, (LANES, LANES), 0) < lax.broadcasted_iota(jnp.int32, (LANES, LANES), 1)
    earlier = jnp.where(earlier, 1.0, 0.0).astype(jnp.bfloat16)
    seen = jnp.zeros((lists, 1), jnp.float32)
    for b in range(ids_ref.shape[1] // LANES):
        hit = ids_ref[:, b * LANES : (b + 1) * LANES] == names
        hot = jnp.where(hit, 1.0, 0.0)
        before = jnp.dot(hot.astype(jnp.bfloat16), earlier, preferred_element_type=jnp.float32) + seen
        key_ref[:, b * LANES : (b + 1) * LANES] = jnp.where(hit, before, -1.0).astype(jnp.int32)
        seen = seen + jnp.sum(hot, axis=1, keepdims=True)
    count_ref[...] = jnp.broadcast_to(seen, count_ref.shape).astype(jnp.int32)


def pack_kernel(first, at, *refs):
    if first:
        names_ref, ids_ref, rows_ref, key_ref, count_ref, *outs = refs
        count_into(key_ref, count_ref, ids_ref)
    else:
        names_ref, rows_ref, key_ref, count_ref, *outs = refs
    cap = outs[0].shape[0]
    slots = lax.broadcasted_iota(jnp.int32, (cap, rows_ref.shape[0]), 0)
    lane = lax.broadcasted_iota(jnp.int32, (cap, LANES), 1)
    slot = lax.broadcasted_iota(jnp.int32, (cap, LANES), 0)
    for k, out_ref in enumerate(outs):
        name = names_ref[at + k]
        pick = jnp.where(key_ref[pl.ds(name, 1), :] == slots, 1.0, 0.0).astype(jnp.bfloat16)
        out = jnp.dot(pick, rows_ref[...], preferred_element_type=jnp.float32)
        out_ref[...] = out.astype(jnp.bfloat16)
        padding = (lane == 0) & (slot >= count_ref[pl.ds(name, 1), :])
        out_ref[:, :LANES] = jnp.where(padding, PAD_MARK, out[:, :LANES]).astype(jnp.bfloat16)


def pack(names, at, blocks, rows, lists, cap, ids=None, keys=None):
    count, width = rows.shape
    made = [jax.ShapeDtypeStruct((cap, width), jnp.bfloat16)] * blocks
    kept = [jax.ShapeDtypeStruct((lists, count), jnp.int32), jax.ShapeDtypeStruct((lists, LANES), jnp.int32)]
    operands = [names] + ([ids, rows] if keys is None else [rows, *keys])
    made = (kept if keys is None else []) + made
    out = pl.pallas_call(
        functools.partial(pack_kernel, keys is None, at),
        out_shape=made,
        in_specs=[SMEM] + [VMEM] * (len(operands) - 1),
        out_specs=[VMEM] * len(made),
        compiler_params=PARAMS,
        cost_estimate=pl.CostEstimate(
            flops=2 * blocks * cap * count * width, bytes_accessed=2 * rows.size, transcendentals=0
        ),
        name="pack",
    )(*operands)
    out = list(out)
    return (out[:2], out[2:]) if keys is None else out


def norm_kernel(cents_ref, *outs):
    for index, out_ref in enumerate(outs):
        c = cents_ref[index].astype(jnp.float32)
        total = jnp.sum(jnp.square(c), axis=1, keepdims=True) * (0.5 * SHARP * LOG2E)
        out_ref[...] = jnp.broadcast_to(total, out_ref.shape)


def norms(cents):
    local, fine, _ = cents.shape
    return pl.pallas_call(
        norm_kernel,
        out_shape=[jax.ShapeDtypeStruct((fine, LANES), jnp.float32)] * local,
        in_specs=[VMEM],
        out_specs=[VMEM] * local,
        compiler_params=PARAMS,
        name="norms",
    )(cents)


def raw_scores(cents_ref, index, rows_ref):
    return lax.dot_general(
        cents_ref[index], rows_ref[...], (((1,), (1,)), ((), ())), preferred_element_type=jnp.float32
    )


def responses(raw, norm_ref, rows_ref):
    cap = rows_ref.shape[0]
    norm = jnp.concatenate([norm_ref[...]] * (cap // LANES), axis=1)
    scores = raw * (SHARP * LOG2E) - norm
    p = jnp.exp2(scores - jnp.max(scores, axis=0, keepdims=True))
    mark = jnp.transpose(rows_ref[:, :LANES].astype(jnp.float32))[0:1, :]
    scale = jnp.where(mark < PAD_TEST, 1.0, 0.0) / jnp.sum(p, axis=0, keepdims=True)
    resp = (p * scale).astype(jnp.bfloat16)
    back = resp.astype(jnp.float32)
    mass = back[:, :LANES]
    for j in range(1, cap // LANES):
        mass = mass + back[:, j * LANES : (j + 1) * LANES]
    return resp, mass


def respond(cents_ref, index, norm_ref, row_refs, all_ref, resp_ref, total):
    raw = raw_scores(cents_ref, index, row_refs[0])
    for n, rows_ref in enumerate(row_refs):
        cap = rows_ref.shape[0]
        now = raw
        if n + 1 < len(row_refs):
            raw = raw_scores(cents_ref, index, row_refs[n + 1])
        all_ref[n * cap : (n + 1) * cap, :] = rows_ref[...]
        resp, mass = responses(now, norm_ref, rows_ref)
        resp_ref[:, n * cap : (n + 1) * cap] = resp
        total = mass if total is None else total + mass
    return total


def stats_kernel(index, blocks, carried, *refs):
    cents_ref, norm_ref = refs[:2]
    row_refs = refs[2 : 2 + blocks]
    sums_ref, mass_ref, all_ref, resp_ref = refs[-4:]
    old = refs[3 + blocks][...] if carried else None
    mass_ref[...] = respond(cents_ref, index, norm_ref, row_refs, all_ref, resp_ref, old)
    size = sums_ref.shape[0] // PIECES
    for at in range(0, sums_ref.shape[0], size):
        part = jnp.dot(resp_ref[at : at + size, :], all_ref[...], preferred_element_type=jnp.float32)
        if carried:
            part = refs[2 + blocks][at : at + size, :] + part
        sums_ref[at : at + size, :] = part


def last_kernel(index, blocks, shares, *refs):
    cents_ref, norm_ref = refs[:2]
    row_refs = refs[2 : 2 + blocks]
    sums_ref, mass_ref, out_ref, old_ref, send_ref, all_ref, resp_ref, in_sem, out_sem = refs[2 + blocks :]
    load = pltpu.make_async_copy(sums_ref, old_ref, in_sem)
    load.start()
    fine, width = old_ref.shape
    share = fine // shares
    groups = width // LANES
    total = respond(cents_ref, index, norm_ref, row_refs, all_ref, resp_ref, mass_ref[...])
    line = jnp.sum(jnp.transpose(total), axis=0, keepdims=True)
    high = line.astype(jnp.bfloat16).astype(jnp.float32)
    low = line - high
    row = lax.broadcasted_iota(jnp.int32, (TAIL_ROWS, LANES), 0)
    load.wait()
    copies = []
    per = shares // PIECES
    for piece in range(PIECES):
        at = piece * per * share
        part = jnp.dot(resp_ref[at : at + per * share, :], all_ref[...], preferred_element_type=jnp.float32)
        part = old_ref[at : at + per * share, :] + part
        for t in range(per):
            s = piece * per + t
            for j in range(groups):
                some = part[t * share : (t + 1) * share, j * LANES : (j + 1) * LANES]
                send_ref[s, j * share : (j + 1) * share, :] = some.astype(jnp.bfloat16)
            where = s * share // LANES * LANES
            both = jnp.where(row == 0, high[:, where : where + LANES], jnp.where(row == 1, low[:, where : where + LANES], 0.0))
            send_ref[s, groups * share :, :] = both.astype(jnp.bfloat16)
        rng = pl.ds(piece * per, per)
        copies.append(pltpu.make_async_copy(send_ref.at[rng], out_ref.at[rng], out_sem.at[piece]))
        copies[-1].start()
    for copy in copies:
        copy.wait()


def stats(cents, index, norm, rows, carried):
    _, fine, width = cents.shape
    sums = jax.ShapeDtypeStruct((fine, width), jnp.float32)
    mass = jax.ShapeDtypeStruct((fine, LANES), jnp.float32)
    count = sum(r.shape[0] for r in rows)
    operands = [cents, norm, *rows, *(carried or ())]
    return pl.pallas_call(
        functools.partial(stats_kernel, index, len(rows), carried is not None),
        out_shape=[sums, mass],
        in_specs=[VMEM] * len(operands),
        out_specs=[VMEM, VMEM],
        scratch_shapes=[pltpu.VMEM((count, width), jnp.bfloat16), pltpu.VMEM((fine, count), jnp.bfloat16)],
        compiler_params=PARAMS,
        name=f"stats_{index}",
    )(*operands)


def last_stats(cents, index, norm, rows, carried, shares):
    _, fine, width = cents.shape
    sent = (shares, fine // shares * (width // LANES) + TAIL_ROWS, LANES)
    count = sum(r.shape[0] for r in rows)
    operands = [cents, norm, *rows, *carried]
    return pl.pallas_call(
        functools.partial(last_kernel, index, len(rows), shares),
        out_shape=jax.ShapeDtypeStruct(sent, jnp.bfloat16),
        in_specs=[VMEM] * (2 + len(rows)) + [pl.BlockSpec(memory_space=pl.ANY), VMEM],
        out_specs=pl.BlockSpec(memory_space=pltpu.HBM),
        scratch_shapes=[
            pltpu.VMEM((fine, width), jnp.float32),
            pltpu.VMEM(sent, jnp.bfloat16),
            pltpu.VMEM((count, width), jnp.bfloat16),
            pltpu.VMEM((fine, count), jnp.bfloat16),
            pltpu.SemaphoreType.DMA,
            pltpu.SemaphoreType.DMA((PIECES,)),
        ],
        compiler_params=PARAMS,
        name=f"last_{index}",
    )(*operands)


def finish_kernel(index, shares, me_ref, got_ref, cents_ref, *rest):
    out_ref, load_ref, own_ref, made_ref, mass_ref, load_sem, own_sem, out_sem = rest[-8:]
    share, width = made_ref.shape
    groups = width // LANES
    ranges = [(groups * share, TAIL_ROWS)] + [(j * share, share) for j in range(groups)]
    loads = []
    for n, (at, size) in enumerate(ranges):
        rng = pl.ds(at, size)
        loads.append(pltpu.make_async_copy(got_ref.at[:, rng, :], load_ref.at[:, rng, :], load_sem.at[n]))
        loads[-1].start()
    first = pl.multiple_of(me_ref[0] * share, share)
    mine = pltpu.make_async_copy(cents_ref.at[index, pl.ds(first, share), :], own_ref, own_sem)
    mine.start()
    loads[0].wait()
    at = groups * share
    tail = load_ref[0, at : at + TAIL_ROWS, :].astype(jnp.float32)
    for k in range(1, shares):
        tail = tail + load_ref[k, at : at + TAIL_ROWS, :].astype(jnp.float32)
    mass_ref[...] = jnp.transpose(jnp.broadcast_to(tail[0:1, :] + tail[1:2, :], (LANES, LANES)))
    offset = pl.multiple_of(lax.rem(me_ref[0] * share, LANES), share)
    scale = 1.0 / (mass_ref[pl.ds(offset, share), :] + PRIOR)
    mine.wait()
    for j in range(groups):
        loads[1 + j].wait()
        at = j * share
        total = PRIOR * own_ref[:, j * LANES : (j + 1) * LANES].astype(jnp.float32)
        for k in range(shares):
            total = total + load_ref[k, at : at + share, :].astype(jnp.float32)
        made_ref[:, j * LANES : (j + 1) * LANES] = total * scale
    store = pltpu.make_async_copy(made_ref, out_ref.at[index], out_sem)
    store.start()
    store.wait()


def finish(me, got, cents, index, sofar):
    local, fine, width = cents.shape
    shares = got.shape[0]
    share = fine // shares
    anywhere = pl.BlockSpec(memory_space=pl.ANY)
    operands = [me, got, cents] + ([] if sofar is None else [sofar])
    return pl.pallas_call(
        functools.partial(finish_kernel, index, shares),
        out_shape=jax.ShapeDtypeStruct((local, share, width), jnp.float32),
        in_specs=[SMEM] + [anywhere] * (len(operands) - 1),
        out_specs=pl.BlockSpec(memory_space=pltpu.HBM),
        scratch_shapes=[
            pltpu.VMEM(got.shape, jnp.bfloat16),
            pltpu.VMEM((share, width), jnp.bfloat16),
            pltpu.VMEM((share, width), jnp.float32),
            pltpu.VMEM((LANES, LANES), jnp.float32),
            pltpu.SemaphoreType.DMA((1 + width // LANES,)),
            pltpu.SemaphoreType.DMA,
            pltpu.SemaphoreType.DMA,
        ],
        input_output_aliases={} if sofar is None else {3: 0},
        compiler_params=PARAMS,
        name=f"finish_{index}",
    )(*operands)


def target(g, step, groups):
    return (g // 2 + step[0]) % (groups // 2) * 2 + (g % 2 ^ step[1])


def hop(block, step, groups):
    if step == (0, 0):
        return block
    return lax.ppermute(block, "list", [(g, target(g, step, groups)) for g in range(groups)])


def per_device(embeddings, list_ids, centroids):
    groups = lax.axis_size("list")
    shares = lax.axis_size("shard")
    local = centroids.shape[0]
    lists = local * groups
    cap = embeddings.shape[0] // 8
    ids = list_ids.reshape(1, -1)
    g = lax.axis_index("list").astype(jnp.int32)
    me = lax.axis_index("shard").astype(jnp.int32).reshape(1)
    table = [[target(k, step, groups) for step in HOPS] for k in range(groups)]
    table = np.array([[d * local + i for i in range(local) for d in row] for row in table], np.int32)
    names = lax.dynamic_index_in_dim(jnp.asarray(table), g, 0, keepdims=False)
    tie = lax.optimization_barrier
    keys, sent = pack(names, 0, FIRST, embeddings, lists, cap, ids=ids)
    sent = sent + pack(names, FIRST, groups - FIRST, embeddings, lists, cap, keys=keys)
    later = []
    for at in range(0, groups, TIED):
        later += pack(names, groups + at, TIED, embeddings, lists, cap, keys=keys)
    sent[-1], later = tie((sent[-1], later))
    norm = norms(centroids)
    rows = [[hop(b, step, groups) for b, step in zip(blocks, HOPS)] for blocks in (sent, later)]
    out, got = None, []
    for index in range(local):
        stages = STAGES[index]
        carried = None
        for stage in stages[:-1]:
            carried = stats(centroids, index, norm[index], [rows[index][k] for k in stage], carried)
        part = last_stats(centroids, index, norm[index], [rows[index][k] for k in stages[-1]], carried, shares)
        if index == 0:
            part, rows[1][:TIED] = tie((part, rows[1][:TIED]))
        else:
            out = finish(me, got[0], centroids, 0, None)
        got.append(lax.all_to_all(part, "shard", split_axis=0, concat_axis=0, tiled=True))
    return finish(me, got[1], centroids, 1, out)


def solution(mesh):
    placed = (P(("list", "shard"), None), P(("list", "shard"), None), P("list", None, None))
    return jax.shard_map(
        per_device, mesh=mesh, in_specs=placed, out_specs=P("list", "shard", None), check_vma=False
    )
```

```python
import functools
import math

import jax
import jax.numpy as jnp
from jax import lax
from jax.experimental import pallas as pl
from jax.experimental.pallas import tpu as pltpu
from jax.sharding import PartitionSpec as P

SHARP = 0.1
PRIOR = 1.0
LOG2E = math.log2(math.e)
LANES = 128
PAD_MARK = 64.0
PAD_TEST = 32.0
TAIL_ROWS = 16
PIECES = 4
HOPS = ((1, 0), (3, 0), (1, 1), (3, 1), (2, 0), (2, 1), (0, 1), (0, 0))
STAGES = (((7, 0, 1), (2, 3, 6), (4, 5)), ((7, 0, 1, 2, 3, 6), (4, 5)))
TIED = 4
FIRST = 2
VMEM = pl.BlockSpec(memory_space=pltpu.VMEM)
SMEM = pl.BlockSpec(memory_space=pltpu.SMEM)
PARAMS = pltpu.CompilerParams(vmem_limit_bytes=20 * 2**20)


def count_into(key_ref, count_ref, ids_ref):
    lists = key_ref.shape[0]
    names = lax.broadcasted_iota(jnp.int32, (lists, LANES), 0)
    earlier = lax.broadcasted_iota(jnp.int32, (LANES, LANES), 0) < lax.broadcasted_iota(jnp.int32, (LANES, LANES), 1)
    earlier = jnp.where(earlier, 1.0, 0.0).astype(jnp.bfloat16)
    seen = jnp.zeros((lists, 1), jnp.float32)
    for b in range(ids_ref.shape[1] // LANES):
        hit = ids_ref[:, b * LANES : (b + 1) * LANES] == names
        hot = jnp.where(hit, 1.0, 0.0)
        before = jnp.dot(hot.astype(jnp.bfloat16), earlier, preferred_element_type=jnp.float32) + seen
        key_ref[:, b * LANES : (b + 1) * LANES] = jnp.where(hit, before, -1.0).astype(jnp.int32)
        seen = seen + jnp.sum(hot, axis=1, keepdims=True)
    count_ref[...] = jnp.broadcast_to(seen, count_ref.shape).astype(jnp.int32)


def pack_kernel(first, hops, index, local, *refs):
    if first:
        ids_ref, rows_hbm, key_ref, count_ref, *outs, rows_ref, sem = refs
        load = pltpu.make_async_copy(rows_hbm, rows_ref, sem)
        load.start()
        count_into(key_ref, count_ref, ids_ref)
    else:
        rows_ref, key_ref, count_ref, *outs = refs
    lists = key_ref.shape[0]
    cap = outs[0].shape[0]
    me = lax.axis_index("list")
    y, core = lax.div(me, 2), lax.rem(me, 2)
    slots = lax.broadcasted_iota(jnp.int32, (cap, rows_ref.shape[0]), 0)
    lane = lax.broadcasted_iota(jnp.int32, (cap, LANES), 1)
    slot = lax.broadcasted_iota(jnp.int32, (cap, LANES), 0)
    if first:
        load.wait()
    for (dy, dc), out_ref in zip(hops, outs):
        to_core = 1 - core if dc else core
        name = (lax.rem(y + dy, lists // local // 2) * 2 + to_core) * local + index
        pick = jnp.where(key_ref[pl.ds(name, 1), :] == slots, 1.0, 0.0).astype(jnp.bfloat16)
        out = jnp.dot(pick, rows_ref[...], preferred_element_type=jnp.float32)
        out_ref[...] = out.astype(jnp.bfloat16)
        padding = (lane == 0) & (slot >= count_ref[pl.ds(name, 1), :])
        out_ref[:, :LANES] = jnp.where(padding, PAD_MARK, out[:, :LANES]).astype(jnp.bfloat16)


def pack(hops, index, local, rows, lists, cap, ids=None, keys=None):
    count, width = rows.shape
    blocks = len(hops)
    made = [jax.ShapeDtypeStruct((cap, width), jnp.bfloat16)] * blocks
    kept = [jax.ShapeDtypeStruct((lists, count), jnp.int32), jax.ShapeDtypeStruct((lists, LANES), jnp.int32)]
    first = keys is None
    operands = [ids, rows] if first else [rows, *keys]
    made = (kept if first else []) + made
    out = pl.pallas_call(
        functools.partial(pack_kernel, first, hops, index, local),
        out_shape=made,
        in_specs=[VMEM, pl.BlockSpec(memory_space=pl.ANY)] if first else [VMEM] * len(operands),
        out_specs=[VMEM] * len(made),
        scratch_shapes=[pltpu.VMEM((count, width), jnp.bfloat16), pltpu.SemaphoreType.DMA] if first else [],
        compiler_params=PARAMS,
        cost_estimate=pl.CostEstimate(
            flops=2 * blocks * cap * count * width, bytes_accessed=2 * rows.size, transcendentals=0
        ),
        name="pack",
    )(*operands)
    out = list(out)
    return (out[:2], out[2:]) if first else out


def norm_kernel(cents_ref, *outs):
    for index, out_ref in enumerate(outs):
        c = cents_ref[index].astype(jnp.float32)
        total = jnp.sum(jnp.square(c), axis=1, keepdims=True) * (0.5 * SHARP * LOG2E)
        out_ref[...] = jnp.broadcast_to(total, out_ref.shape)


def norms(cents):
    local, fine, _ = cents.shape
    return pl.pallas_call(
        norm_kernel,
        out_shape=[jax.ShapeDtypeStruct((fine, LANES), jnp.float32)] * local,
        in_specs=[VMEM],
        out_specs=[VMEM] * local,
        compiler_params=PARAMS,
        name="norms",
    )(cents)


def raw_scores(cents_ref, index, rows_ref):
    return lax.dot_general(
        cents_ref[index], rows_ref[...], (((1,), (1,)), ((), ())), preferred_element_type=jnp.float32
    )


def responses(raw, norm_ref, rows_ref):
    cap = rows_ref.shape[0]
    norm = jnp.concatenate([norm_ref[...]] * (cap // LANES), axis=1)
    scores = raw * (SHARP * LOG2E) - norm
    p = jnp.exp2(scores - jnp.max(scores, axis=0, keepdims=True))
    mark = jnp.transpose(rows_ref[:, :LANES].astype(jnp.float32))[0:1, :]
    scale = jnp.where(mark < PAD_TEST, 1.0, 0.0) / jnp.sum(p, axis=0, keepdims=True)
    resp = (p * scale).astype(jnp.bfloat16)
    back = resp.astype(jnp.float32)
    mass = back[:, :LANES]
    for j in range(1, cap // LANES):
        mass = mass + back[:, j * LANES : (j + 1) * LANES]
    return resp, mass


def respond(cents_ref, index, norm_ref, row_refs, all_ref, resp_ref, total):
    raw = raw_scores(cents_ref, index, row_refs[0])
    for n, rows_ref in enumerate(row_refs):
        cap = rows_ref.shape[0]
        now = raw
        if n + 1 < len(row_refs):
            raw = raw_scores(cents_ref, index, row_refs[n + 1])
        all_ref[n * cap : (n + 1) * cap, :] = rows_ref[...]
        resp, mass = responses(now, norm_ref, rows_ref)
        resp_ref[:, n * cap : (n + 1) * cap] = resp
        total = mass if total is None else total + mass
    return total


def stats_kernel(index, blocks, carried, *refs):
    cents_ref, norm_ref = refs[:2]
    row_refs = refs[2 : 2 + blocks]
    sums_ref, mass_ref, all_ref, resp_ref = refs[-4:]
    old = refs[3 + blocks][...] if carried else None
    mass_ref[...] = respond(cents_ref, index, norm_ref, row_refs, all_ref, resp_ref, old)
    size = sums_ref.shape[0] // PIECES
    for at in range(0, sums_ref.shape[0], size):
        part = jnp.dot(resp_ref[at : at + size, :], all_ref[...], preferred_element_type=jnp.float32)
        if carried:
            part = refs[2 + blocks][at : at + size, :] + part
        sums_ref[at : at + size, :] = part


def last_kernel(index, blocks, shares, *refs):
    cents_ref, norm_ref = refs[:2]
    row_refs = refs[2 : 2 + blocks]
    sums_ref, mass_ref, out_ref, old_ref, send_ref, all_ref, resp_ref, in_sem, out_sem = refs[2 + blocks :]
    load = pltpu.make_async_copy(sums_ref, old_ref, in_sem)
    load.start()
    fine, width = old_ref.shape
    share = fine // shares
    groups = width // LANES
    total = respond(cents_ref, index, norm_ref, row_refs, all_ref, resp_ref, mass_ref[...])
    line = jnp.sum(jnp.transpose(total), axis=0, keepdims=True)
    high = line.astype(jnp.bfloat16).astype(jnp.float32)
    low = line - high
    row = lax.broadcasted_iota(jnp.int32, (TAIL_ROWS, LANES), 0)
    load.wait()
    copies = []
    per = shares // PIECES
    for piece in range(PIECES):
        at = piece * per * share
        part = jnp.dot(resp_ref[at : at + per * share, :], all_ref[...], preferred_element_type=jnp.float32)
        part = old_ref[at : at + per * share, :] + part
        for t in range(per):
            s = piece * per + t
            for j in range(groups):
                some = part[t * share : (t + 1) * share, j * LANES : (j + 1) * LANES]
                send_ref[s, j * share : (j + 1) * share, :] = some.astype(jnp.bfloat16)
            where = s * share // LANES * LANES
            both = jnp.where(row == 0, high[:, where : where + LANES], jnp.where(row == 1, low[:, where : where + LANES], 0.0))
            send_ref[s, groups * share :, :] = both.astype(jnp.bfloat16)
        rng = pl.ds(piece * per, per)
        copies.append(pltpu.make_async_copy(send_ref.at[rng], out_ref.at[rng], out_sem.at[piece]))
        copies[-1].start()
    for copy in copies:
        copy.wait()


def stats(cents, index, norm, rows, carried):
    _, fine, width = cents.shape
    sums = jax.ShapeDtypeStruct((fine, width), jnp.float32)
    mass = jax.ShapeDtypeStruct((fine, LANES), jnp.float32)
    count = sum(r.shape[0] for r in rows)
    operands = [cents, norm, *rows, *(carried or ())]
    return pl.pallas_call(
        functools.partial(stats_kernel, index, len(rows), carried is not None),
        out_shape=[sums, mass],
        in_specs=[VMEM] * len(operands),
        out_specs=[VMEM, VMEM],
        scratch_shapes=[pltpu.VMEM((count, width), jnp.bfloat16), pltpu.VMEM((fine, count), jnp.bfloat16)],
        compiler_params=PARAMS,
        name=f"stats_{index}",
    )(*operands)


def last_stats(cents, index, norm, rows, carried, shares):
    _, fine, width = cents.shape
    sent = (shares, fine // shares * (width // LANES) + TAIL_ROWS, LANES)
    count = sum(r.shape[0] for r in rows)
    operands = [cents, norm, *rows, *carried]
    return pl.pallas_call(
        functools.partial(last_kernel, index, len(rows), shares),
        out_shape=pltpu.HBM(sent, jnp.bfloat16),
        in_specs=[VMEM] * (2 + len(rows)) + [pl.BlockSpec(memory_space=pl.ANY), VMEM],
        out_specs=pl.BlockSpec(memory_space=pltpu.HBM),
        scratch_shapes=[
            pltpu.VMEM((fine, width), jnp.float32),
            pltpu.VMEM(sent, jnp.bfloat16),
            pltpu.VMEM((count, width), jnp.bfloat16),
            pltpu.VMEM((fine, count), jnp.bfloat16),
            pltpu.SemaphoreType.DMA,
            pltpu.SemaphoreType.DMA((PIECES,)),
        ],
        compiler_params=PARAMS,
        name=f"last_{index}",
    )(*operands)


def finish_kernel(index, shares, me_ref, got_ref, cents_ref, *rest):
    out_ref, load_ref, own_ref, made_ref, mass_ref, load_sem, own_sem, out_sem = rest[-8:]
    share, width = made_ref.shape
    groups = width // LANES
    ranges = [(groups * share, TAIL_ROWS)] + [(j * share, share) for j in range(groups)]
    loads = []
    for n, (at, size) in enumerate(ranges):
        rng = pl.ds(at, size)
        loads.append(pltpu.make_async_copy(got_ref.at[:, rng, :], load_ref.at[:, rng, :], load_sem.at[n]))
        loads[-1].start()
    first = pl.multiple_of(me_ref[0] * share, share)
    mine = pltpu.make_async_copy(cents_ref.at[index, pl.ds(first, share), :], own_ref, own_sem)
    mine.start()
    loads[0].wait()
    at = groups * share
    tail = load_ref[0, at : at + TAIL_ROWS, :].astype(jnp.float32)
    for k in range(1, shares):
        tail = tail + load_ref[k, at : at + TAIL_ROWS, :].astype(jnp.float32)
    mass_ref[...] = jnp.transpose(jnp.broadcast_to(tail[0:1, :] + tail[1:2, :], (LANES, LANES)))
    offset = pl.multiple_of(lax.rem(me_ref[0] * share, LANES), share)
    scale = 1.0 / (mass_ref[pl.ds(offset, share), :] + PRIOR)
    mine.wait()
    for j in range(groups):
        loads[1 + j].wait()
        at = j * share
        total = PRIOR * own_ref[:, j * LANES : (j + 1) * LANES].astype(jnp.float32)
        for k in range(shares):
            total = total + load_ref[k, at : at + share, :].astype(jnp.float32)
        made_ref[:, j * LANES : (j + 1) * LANES] = total * scale
    store = pltpu.make_async_copy(made_ref, out_ref.at[index], out_sem)
    store.start()
    store.wait()


def finish(me, got, cents, index, sofar):
    local, fine, width = cents.shape
    shares = got.shape[0]
    share = fine // shares
    anywhere = pl.BlockSpec(memory_space=pl.ANY)
    operands = [me, got, cents] + ([] if sofar is None else [sofar])
    return pl.pallas_call(
        functools.partial(finish_kernel, index, shares),
        out_shape=jax.ShapeDtypeStruct((local, share, width), jnp.float32),
        in_specs=[SMEM] + [anywhere] * (len(operands) - 1),
        out_specs=pl.BlockSpec(memory_space=pltpu.HBM),
        scratch_shapes=[
            pltpu.VMEM(got.shape, jnp.bfloat16),
            pltpu.VMEM((share, width), jnp.bfloat16),
            pltpu.VMEM((share, width), jnp.float32),
            pltpu.VMEM((LANES, LANES), jnp.float32),
            pltpu.SemaphoreType.DMA((1 + width // LANES,)),
            pltpu.SemaphoreType.DMA,
            pltpu.SemaphoreType.DMA,
        ],
        input_output_aliases={} if sofar is None else {3: 0},
        compiler_params=PARAMS,
        name=f"finish_{index}",
    )(*operands)


def target(g, step, groups):
    return (g // 2 + step[0]) % (groups // 2) * 2 + (g % 2 ^ step[1])


def hop(block, step, groups):
    if step == (0, 0):
        return block
    return lax.ppermute(block, "list", [(g, target(g, step, groups)) for g in range(groups)])


def per_device(embeddings, list_ids, centroids):
    groups = lax.axis_size("list")
    shares = lax.axis_size("shard")
    local = centroids.shape[0]
    lists = local * groups
    cap = embeddings.shape[0] // 8
    ids = list_ids.reshape(1, -1)
    me = lax.axis_index("shard").astype(jnp.int32).reshape(1)
    tie = lax.optimization_barrier
    keys, sent = pack(HOPS[:FIRST], 0, local, embeddings, lists, cap, ids=ids)
    sent += pack(HOPS[FIRST:], 0, local, embeddings, lists, cap, keys=keys)
    later = []
    for at in range(0, groups, TIED):
        later += pack(HOPS[at : at + TIED], 1, local, embeddings, lists, cap, keys=keys)
    sent[-1], later = tie((sent[-1], later))
    norm = norms(centroids)
    rows = [[hop(b, step, groups) for b, step in zip(blocks, HOPS)] for blocks in (sent, later)]
    out, got = None, []
    for index in range(local):
        stages = STAGES[index]
        carried = None
        for stage in stages[:-1]:
            carried = stats(centroids, index, norm[index], [rows[index][k] for k in stage], carried)
        part = last_stats(centroids, index, norm[index], [rows[index][k] for k in stages[-1]], carried, shares)
        if index == 0:
            part, rows[1][:TIED] = tie((part, rows[1][:TIED]))
        else:
            out = finish(me, got[0], centroids, 0, None)
        got.append(lax.all_to_all(part, "shard", split_axis=0, concat_axis=0, tiled=True))
    return finish(me, got[1], centroids, 1, out)


def solution(mesh):
    placed = (P(("list", "shard"), None), P(("list", "shard"), None), P("list", None, None))
    return jax.shard_map(
        per_device, mesh=mesh, in_specs=placed, out_specs=P("list", "shard", None), check_vma=False
    )
```

```python
import functools
import math

import jax
import jax.numpy as jnp
from jax import lax
from jax.experimental import pallas as pl
from jax.experimental.pallas import tpu as pltpu
from jax.sharding import PartitionSpec as P

SHARP = 0.1
PRIOR = 1.0
LOG2E = math.log2(math.e)
LANES = 128
PAD_MARK = 64.0
PAD_TEST = 32.0
TAIL_ROWS = 16
PIECES = 4
HOPS = ((2, 0), (2, 1), (1, 0), (3, 0), (1, 1), (3, 1), (0, 1), (0, 0))
STAGES = (((7, 0, 1), (2, 3, 6), (4, 5)), ((7, 0, 1), (2, 3, 6), (4, 5)))
TIED = 2
FIRST = 2
VMEM = pl.BlockSpec(memory_space=pltpu.VMEM)
SMEM = pl.BlockSpec(memory_space=pltpu.SMEM)
PARAMS = pltpu.CompilerParams(vmem_limit_bytes=20 * 2**20)


def count_into(key_ref, count_ref, ids_ref):
    lists = key_ref.shape[0]
    names = lax.broadcasted_iota(jnp.int32, (lists, LANES), 0)
    earlier = lax.broadcasted_iota(jnp.int32, (LANES, LANES), 0) < lax.broadcasted_iota(jnp.int32, (LANES, LANES), 1)
    earlier = jnp.where(earlier, 1.0, 0.0).astype(jnp.bfloat16)
    seen = jnp.zeros((lists, 1), jnp.float32)
    for b in range(ids_ref.shape[1] // LANES):
        hit = ids_ref[:, b * LANES : (b + 1) * LANES] == names
        hot = jnp.where(hit, 1.0, 0.0)
        before = jnp.dot(hot.astype(jnp.bfloat16), earlier, preferred_element_type=jnp.float32) + seen
        key_ref[:, b * LANES : (b + 1) * LANES] = jnp.where(hit, before, -1.0).astype(jnp.int32)
        seen = seen + jnp.sum(hot, axis=1, keepdims=True)
    count_ref[...] = jnp.broadcast_to(seen, count_ref.shape).astype(jnp.int32)


def pack_kernel(first, hops, index, local, *refs):
    if first:
        ids_ref, rows_hbm, key_ref, count_ref, *outs, rows_ref, sem = refs
        load = pltpu.make_async_copy(rows_hbm, rows_ref, sem)
        load.start()
        count_into(key_ref, count_ref, ids_ref)
    else:
        rows_ref, key_ref, count_ref, *outs = refs
    lists = key_ref.shape[0]
    cap = outs[0].shape[0]
    me = lax.axis_index("list")
    y, core = lax.div(me, 2), lax.rem(me, 2)
    slots = lax.broadcasted_iota(jnp.int32, (cap, rows_ref.shape[0]), 0)
    lane = lax.broadcasted_iota(jnp.int32, (cap, LANES), 1)
    slot = lax.broadcasted_iota(jnp.int32, (cap, LANES), 0)
    if first:
        load.wait()
    for (dy, dc), out_ref in zip(hops, outs):
        to_core = 1 - core if dc else core
        name = (lax.rem(y + dy, lists // local // 2) * 2 + to_core) * local + index
        pick = jnp.where(key_ref[pl.ds(name, 1), :] == slots, 1.0, 0.0).astype(jnp.bfloat16)
        out = jnp.dot(pick, rows_ref[...], preferred_element_type=jnp.float32)
        out_ref[...] = out.astype(jnp.bfloat16)
        padding = (lane == 0) & (slot >= count_ref[pl.ds(name, 1), :])
        out_ref[:, :LANES] = jnp.where(padding, PAD_MARK, out[:, :LANES]).astype(jnp.bfloat16)


def pack(hops, index, local, rows, lists, cap, ids=None, keys=None):
    count, width = rows.shape
    blocks = len(hops)
    made = [jax.ShapeDtypeStruct((cap, width), jnp.bfloat16)] * blocks
    kept = [jax.ShapeDtypeStruct((lists, count), jnp.int32), jax.ShapeDtypeStruct((lists, LANES), jnp.int32)]
    first = keys is None
    operands = [ids, pltpu.with_memory_space_constraint(rows, pltpu.HBM)] if first else [rows, *keys]
    made = (kept if first else []) + made
    out = pl.pallas_call(
        functools.partial(pack_kernel, first, hops, index, local),
        out_shape=made,
        in_specs=[VMEM, pl.BlockSpec(memory_space=pltpu.HBM)] if first else [VMEM] * len(operands),
        out_specs=[VMEM] * len(made),
        scratch_shapes=[pltpu.VMEM((count, width), jnp.bfloat16), pltpu.SemaphoreType.DMA] if first else [],
        compiler_params=PARAMS,
        cost_estimate=pl.CostEstimate(
            flops=2 * blocks * cap * count * width, bytes_accessed=2 * rows.size, transcendentals=0
        ),
        name="pack",
    )(*operands)
    out = list(out)
    return (out[:2], out[2:]) if first else out


def norm_kernel(cents_ref, *outs):
    for index, out_ref in enumerate(outs):
        c = cents_ref[index].astype(jnp.float32)
        total = jnp.sum(jnp.square(c), axis=1, keepdims=True) * (0.5 * SHARP * LOG2E)
        out_ref[...] = jnp.broadcast_to(total, out_ref.shape)


def norms(cents):
    local, fine, _ = cents.shape
    return pl.pallas_call(
        norm_kernel,
        out_shape=[jax.ShapeDtypeStruct((fine, LANES), jnp.float32)] * local,
        in_specs=[VMEM],
        out_specs=[VMEM] * local,
        compiler_params=PARAMS,
        name="norms",
    )(cents)


def raw_scores(cents_ref, index, rows_ref):
    return lax.dot_general(
        cents_ref[index], rows_ref[...], (((1,), (1,)), ((), ())), preferred_element_type=jnp.float32
    )


def responses(raw, norm_ref, rows_ref):
    cap = rows_ref.shape[0]
    norm = jnp.concatenate([norm_ref[...]] * (cap // LANES), axis=1)
    scores = raw * (SHARP * LOG2E) - norm
    p = jnp.exp2(scores - jnp.max(scores, axis=0, keepdims=True))
    mark = jnp.transpose(rows_ref[:, :LANES].astype(jnp.float32))[0:1, :]
    scale = jnp.where(mark < PAD_TEST, 1.0, 0.0) / jnp.sum(p, axis=0, keepdims=True)
    resp = (p * scale).astype(jnp.bfloat16)
    back = resp.astype(jnp.float32)
    mass = back[:, :LANES]
    for j in range(1, cap // LANES):
        mass = mass + back[:, j * LANES : (j + 1) * LANES]
    return resp, mass


def respond(cents_ref, index, norm_ref, row_refs, all_ref, resp_ref, total):
    raw = raw_scores(cents_ref, index, row_refs[0])
    for n, rows_ref in enumerate(row_refs):
        cap = rows_ref.shape[0]
        now = raw
        if n + 1 < len(row_refs):
            raw = raw_scores(cents_ref, index, row_refs[n + 1])
        all_ref[n * cap : (n + 1) * cap, :] = rows_ref[...]
        resp, mass = responses(now, norm_ref, rows_ref)
        resp_ref[:, n * cap : (n + 1) * cap] = resp
        total = mass if total is None else total + mass
    return total


def stats_kernel(index, blocks, carried, *refs):
    cents_ref, norm_ref = refs[:2]
    row_refs = refs[2 : 2 + blocks]
    sums_ref, mass_ref, all_ref, resp_ref = refs[-4:]
    old = refs[3 + blocks][...] if carried else None
    mass_ref[...] = respond(cents_ref, index, norm_ref, row_refs, all_ref, resp_ref, old)
    size = sums_ref.shape[0] // PIECES
    for at in range(0, sums_ref.shape[0], size):
        part = jnp.dot(resp_ref[at : at + size, :], all_ref[...], preferred_element_type=jnp.float32)
        if carried:
            part = refs[2 + blocks][at : at + size, :] + part
        sums_ref[at : at + size, :] = part


def last_kernel(index, blocks, shares, *refs):
    cents_ref, norm_ref = refs[:2]
    row_refs = refs[2 : 2 + blocks]
    sums_ref, mass_ref, out_ref, old_ref, send_ref, all_ref, resp_ref, in_sem, out_sem = refs[2 + blocks :]
    load = pltpu.make_async_copy(sums_ref, old_ref, in_sem)
    load.start()
    fine, width = old_ref.shape
    share = fine // shares
    groups = width // LANES
    total = respond(cents_ref, index, norm_ref, row_refs, all_ref, resp_ref, mass_ref[...])
    line = jnp.sum(jnp.transpose(total), axis=0, keepdims=True)
    high = line.astype(jnp.bfloat16).astype(jnp.float32)
    low = line - high
    row = lax.broadcasted_iota(jnp.int32, (TAIL_ROWS, LANES), 0)
    load.wait()
    copies = []
    per = shares // PIECES
    for piece in range(PIECES):
        at = piece * per * share
        part = jnp.dot(resp_ref[at : at + per * share, :], all_ref[...], preferred_element_type=jnp.float32)
        part = old_ref[at : at + per * share, :] + part
        for t in range(per):
            s = piece * per + t
            for j in range(groups):
                some = part[t * share : (t + 1) * share, j * LANES : (j + 1) * LANES]
                send_ref[s, j * share : (j + 1) * share, :] = some.astype(jnp.bfloat16)
            where = s * share // LANES * LANES
            both = jnp.where(row == 0, high[:, where : where + LANES], jnp.where(row == 1, low[:, where : where + LANES], 0.0))
            send_ref[s, groups * share :, :] = both.astype(jnp.bfloat16)
        rng = pl.ds(piece * per, per)
        copies.append(pltpu.make_async_copy(send_ref.at[rng], out_ref.at[rng], out_sem.at[piece]))
        copies[-1].start()
    for copy in copies:
        copy.wait()


def stats(cents, index, norm, rows, carried):
    _, fine, width = cents.shape
    sums = jax.ShapeDtypeStruct((fine, width), jnp.float32)
    mass = jax.ShapeDtypeStruct((fine, LANES), jnp.float32)
    count = sum(r.shape[0] for r in rows)
    operands = [cents, norm, *rows, *(carried or ())]
    return pl.pallas_call(
        functools.partial(stats_kernel, index, len(rows), carried is not None),
        out_shape=[sums, mass],
        in_specs=[VMEM] * len(operands),
        out_specs=[VMEM, VMEM],
        scratch_shapes=[pltpu.VMEM((count, width), jnp.bfloat16), pltpu.VMEM((fine, count), jnp.bfloat16)],
        compiler_params=PARAMS,
        name=f"stats_{index}",
    )(*operands)


def last_stats(cents, index, norm, rows, carried, shares):
    _, fine, width = cents.shape
    sent = (shares, fine // shares * (width // LANES) + TAIL_ROWS, LANES)
    count = sum(r.shape[0] for r in rows)
    operands = [cents, norm, *rows, *carried]
    return pl.pallas_call(
        functools.partial(last_kernel, index, len(rows), shares),
        out_shape=pltpu.HBM(sent, jnp.bfloat16),
        in_specs=[VMEM] * (2 + len(rows)) + [pl.BlockSpec(memory_space=pl.ANY), VMEM],
        out_specs=pl.BlockSpec(memory_space=pltpu.HBM),
        scratch_shapes=[
            pltpu.VMEM((fine, width), jnp.float32),
            pltpu.VMEM(sent, jnp.bfloat16),
            pltpu.VMEM((count, width), jnp.bfloat16),
            pltpu.VMEM((fine, count), jnp.bfloat16),
            pltpu.SemaphoreType.DMA,
            pltpu.SemaphoreType.DMA((PIECES,)),
        ],
        compiler_params=PARAMS,
        name=f"last_{index}",
    )(*operands)


def finish_kernel(index, shares, me_ref, got_ref, cents_ref, *rest):
    out_ref, load_ref, own_ref, made_ref, mass_ref, load_sem, own_sem, out_sem = rest[-8:]
    share, width = made_ref.shape
    groups = width // LANES
    ranges = [(groups * share, TAIL_ROWS)] + [(j * share, share) for j in range(groups)]
    loads = []
    for n, (at, size) in enumerate(ranges):
        rng = pl.ds(at, size)
        loads.append(pltpu.make_async_copy(got_ref.at[:, rng, :], load_ref.at[:, rng, :], load_sem.at[n]))
        loads[-1].start()
    first = pl.multiple_of(me_ref[0] * share, share)
    mine = pltpu.make_async_copy(cents_ref.at[index, pl.ds(first, share), :], own_ref, own_sem)
    mine.start()
    loads[0].wait()
    at = groups * share
    tail = load_ref[0, at : at + TAIL_ROWS, :].astype(jnp.float32)
    for k in range(1, shares):
        tail = tail + load_ref[k, at : at + TAIL_ROWS, :].astype(jnp.float32)
    mass_ref[...] = jnp.transpose(jnp.broadcast_to(tail[0:1, :] + tail[1:2, :], (LANES, LANES)))
    offset = pl.multiple_of(lax.rem(me_ref[0] * share, LANES), share)
    scale = 1.0 / (mass_ref[pl.ds(offset, share), :] + PRIOR)
    mine.wait()
    for j in range(groups):
        loads[1 + j].wait()
        at = j * share
        total = PRIOR * own_ref[:, j * LANES : (j + 1) * LANES].astype(jnp.float32)
        for k in range(shares):
            total = total + load_ref[k, at : at + share, :].astype(jnp.float32)
        made_ref[:, j * LANES : (j + 1) * LANES] = total * scale
    store = pltpu.make_async_copy(made_ref, out_ref.at[index], out_sem)
    store.start()
    store.wait()


def finish(me, got, cents, index, sofar):
    local, fine, width = cents.shape
    shares = got.shape[0]
    share = fine // shares
    anywhere = pl.BlockSpec(memory_space=pl.ANY)
    operands = [me, got, cents] + ([] if sofar is None else [sofar])
    return pl.pallas_call(
        functools.partial(finish_kernel, index, shares),
        out_shape=jax.ShapeDtypeStruct((local, share, width), jnp.float32),
        in_specs=[SMEM] + [anywhere] * (len(operands) - 1),
        out_specs=pl.BlockSpec(memory_space=pltpu.HBM),
        scratch_shapes=[
            pltpu.VMEM(got.shape, jnp.bfloat16),
            pltpu.VMEM((share, width), jnp.bfloat16),
            pltpu.VMEM((share, width), jnp.float32),
            pltpu.VMEM((LANES, LANES), jnp.float32),
            pltpu.SemaphoreType.DMA((1 + width // LANES,)),
            pltpu.SemaphoreType.DMA,
            pltpu.SemaphoreType.DMA,
        ],
        input_output_aliases={} if sofar is None else {3: 0},
        compiler_params=PARAMS,
        name=f"finish_{index}",
    )(*operands)


def target(g, step, groups):
    return (g // 2 + step[0]) % (groups // 2) * 2 + (g % 2 ^ step[1])


def hop(block, step, groups):
    if step == (0, 0):
        return block
    return lax.ppermute(block, "list", [(g, target(g, step, groups)) for g in range(groups)])


def per_device(embeddings, list_ids, centroids):
    groups = lax.axis_size("list")
    shares = lax.axis_size("shard")
    local = centroids.shape[0]
    lists = local * groups
    cap = embeddings.shape[0] // 8
    ids = list_ids.reshape(1, -1)
    me = lax.axis_index("shard").astype(jnp.int32).reshape(1)
    tie = lax.optimization_barrier
    keys, sent = pack(HOPS[:FIRST], 0, local, embeddings, lists, cap, ids=ids)
    sent += pack(HOPS[FIRST:], 0, local, embeddings, lists, cap, keys=keys)
    later = []
    for at in range(0, groups, 4):
        later += pack(HOPS[at : at + 4], 1, local, embeddings, lists, cap, keys=keys)
    sent[-1], later = tie((sent[-1], later))
    norm = norms(centroids)
    rows = [[hop(b, step, groups) for b, step in zip(blocks, HOPS)] for blocks in (sent, later)]
    out, got = None, []
    for index in range(local):
        stages = STAGES[index]
        carried = None
        for stage in stages[:-1]:
            carried = stats(centroids, index, norm[index], [rows[index][k] for k in stage], carried)
        part = last_stats(centroids, index, norm[index], [rows[index][k] for k in stages[-1]], carried, shares)
        if index == 0:
            part, rows[1][:TIED] = tie((part, rows[1][:TIED]))
        else:
            out = finish(me, got[0], centroids, 0, None)
        got.append(lax.all_to_all(part, "shard", split_axis=0, concat_axis=0, tiled=True))
    return finish(me, got[1], centroids, 1, out)


def solution(mesh):
    placed = (P(("list", "shard"), None), P(("list", "shard"), None), P("list", None, None))
    return jax.shard_map(
        per_device, mesh=mesh, in_specs=placed, out_specs=P("list", "shard", None), check_vma=False
    )
```
